32 devices in a mesh: fsdp: 4 (over y, x), ctx: 8 (over z, core).
Axes of the slice: x: 2, y: 2, z: 4, core: 2. Of those that a mesh axis runs over, the one named last changes fastest.
Arguments:
- tokens: bfloat16 [4, 1024, 960], P('fsdp', 'ctx'), may hold values from -6 to 6
- positions: int32 [4, 1024], P('fsdp', 'ctx'), may hold values from 0 to 1023, as said below
- cotangent: bfloat16 [4, 1024, 960], P('fsdp', 'ctx'), may hold values from -6 to 6
- w_query: bfloat16 [2, 960, 960], P(None, 'fsdp'), may hold values from -0.1875 to 0.1875
- w_key: bfloat16 [2, 960, 320], P(None, 'fsdp'), may hold values from -0.1875 to 0.1875
- w_value: bfloat16 [2, 960, 320], P(None, 'fsdp'), may hold values from -0.1875 to 0.1875
- w_out: bfloat16 [2, 960, 960], P(None, 'fsdp'), may hold values from -1 to 1
- w_gate: bfloat16 [2, 960, 2560], P(None, 'fsdp'), may hold values from -0.1875 to 0.1875
- w_up: bfloat16 [2, 960, 2560], P(None, 'fsdp'), may hold values from -0.1875 to 0.1875
- w_down: bfloat16 [2, 2560, 960], P(None, 'fsdp'), may hold values from -0.125 to 0.125
- gain_attn: bfloat16 [2, 960], P(None, 'fsdp'), may hold values from 0.5 to 1.5
- gain_mlp: bfloat16 [2, 960], P(None, 'fsdp'), may hold values from 0.5 to 1.5
Outputs:
- output: bfloat16 [4, 1024, 960], P('fsdp', 'ctx')
- grad_tokens: bfloat16 [4, 1024, 960], P('fsdp', 'ctx')
- grad_query: float32 [2, 960, 960], P(None, 'fsdp')
- grad_key: float32 [2, 960, 320], P(None, 'fsdp')
- grad_value: float32 [2, 960, 320], P(None, 'fsdp')
- grad_out: float32 [2, 960, 960], P(None, 'fsdp')
- grad_gate: float32 [2, 960, 2560], P(None, 'fsdp')
- grad_up: float32 [2, 960, 2560], P(None, 'fsdp')
- grad_down: float32 [2, 2560, 960], P(None, 'fsdp')
- grad_gain_attn: float32 [2, 960], P(None, 'fsdp')
- grad_gain_mlp: float32 [2, 960], P(None, 'fsdp')
The draws below stay inside these ranges and needn't reach their ends.
Inputs may be any that keep to these rules, and one draw needn't show every extreme that they name: Row s lists the positions of sequence s in the order of its tokens: a permutation of 0 to 1023 made of whole blocks of 64 consecutive positions in ascending order; the 128 tokens of one index of ctx are block b followed by block 15 - b.
All inputs are finite; a program needn't handle non-finite values.
Results may differ from the reference program's by a relative error of at most 0.03.
Values may be sent and summed in bfloat16 or wider, within the bound.
A program may use at most 384 MiB of HBM per device.

```python
import jax
import jax.numpy as jnp
from jax import lax

D = 960
QUERY_HEADS = 15
KEY_VALUE_HEADS = 5
HEAD_SIZE = 64
FF = 2560
LAYERS = 2
BLK = 64
QW = 960
KVW = 320
BLOCKS = 16
SEQ_LEN = 1024
SEQS = 4
N_FSDP = 4
N_CTX = 8


def draw_positions(key, part):
    key = jax.random.fold_in(key, 7)
    key_rows = jax.random.split(key, N_FSDP)
    order = jax.vmap(lambda item: jax.random.permutation(item, N_CTX))(key_rows).astype(jnp.int32)
    inner = jnp.arange(BLK, dtype=jnp.int32)
    first = order[:, :, None] * BLK + inner[None, None, :]
    second = (BLOCKS - 1 - order)[:, :, None] * BLK + inner[None, None, :]
    return jnp.concatenate([first, second], axis=2).reshape(N_FSDP, SEQ_LEN).astype(jnp.int32)


def block_levels(key, shape, cuts, low, high):
    level = 1.0
    for axis_at, parts in cuts:
        heights = jax.random.uniform(jax.random.fold_in(jax.random.fold_in(key, 6), axis_at), (parts,), jnp.float32, low / len(cuts), high / len(cuts))
        level = level * jnp.repeat(jnp.exp(heights), shape[axis_at] // parts).reshape((-1,) + (1,) * (len(shape) - 1 - axis_at))
    return level


def gaussian(own_key, extent, deviation, reach, shards=(), kind=jnp.bfloat16):
    entries = deviation * jax.random.normal(own_key, extent, jnp.float32)
    if shards:
        entries = entries * block_levels(own_key, extent, shards, -0.22, 0.18)
    return jnp.clip(entries, -reach, reach).astype(kind)


def setup_inputs(seed: int = 0) -> dict:
    key_of = jax.random.split(jax.random.key(seed), 13)
    return {
        "tokens": gaussian(key_of[0], (SEQS, SEQ_LEN, D), 1.0, 6.0, ((0, 4), (1, 8))),
        "positions": draw_positions(jax.random.fold_in(key_of[12], 71), 0),
        "cotangent": gaussian(key_of[2], (SEQS, SEQ_LEN, D), 1.0, 6.0, ((0, 4), (1, 8))),
        "w_query": gaussian(key_of[3], (LAYERS, D, QW), D ** -0.5, 0.1875, ((1, 4),)),
        "w_key": gaussian(key_of[4], (LAYERS, D, KVW), D ** -0.5, 0.1875, ((1, 4),)),
        "w_value": gaussian(key_of[5], (LAYERS, D, KVW), D ** -0.5, 0.1875, ((1, 4),)),
        "w_out": gaussian(key_of[6], (LAYERS, QW, D), (QW // 32) ** -0.5, 1.0, ((1, 4),)),
        "w_gate": gaussian(key_of[7], (LAYERS, D, FF), D ** -0.5, 0.1875, ((1, 4),)),
        "w_up": gaussian(key_of[8], (LAYERS, D, FF), D ** -0.5, 0.1875, ((1, 4),)),
        "w_down": gaussian(key_of[9], (LAYERS, FF, D), FF ** -0.5, 0.125, ((1, 4),)),
        "gain_attn": jnp.clip(1.0 + 0.1 * jax.random.normal(key_of[10], (LAYERS, D), jnp.float32), 0.5, 1.5).astype(jnp.bfloat16),
        "gain_mlp": jnp.clip(1.0 + 0.1 * jax.random.normal(key_of[11], (LAYERS, D), jnp.float32), 0.5, 1.5).astype(jnp.bfloat16),
    }


EPS = 1e-05
ROPE_BASE = 100000.0
SCORE_FLOOR = -1e+30
HIGH = lax.Precision.HIGHEST

@jax.custom_vjp
def lower_half(v):
    return lax.optimization_barrier(v.astype(jnp.bfloat16)).astype(jnp.float32)

@jax.custom_vjp
def lower_half_backward(v):
    return v

def low_keep(v):
    return (lower_half(v), None)

def low_pass(kept, grad):
    return (grad,)

def back_keep(v):
    return (v, None)

def back_low(kept, grad):
    return (lower_half(grad),)
lower_half.defvjp(low_keep, low_pass)
lower_half_backward.defvjp(back_keep, back_low)

def rms_scale(hidden, gain):
    return hidden * lax.rsqrt(lax.optimization_barrier(jnp.mean(hidden * hidden, axis=-1, keepdims=True)) + EPS) * gain

def rope_tables(token_positions):
    half = HEAD_SIZE // 2
    freqs = ROPE_BASE ** (-jnp.arange(half, dtype=jnp.float32) * 2.0 / HEAD_SIZE)
    angles = token_positions.astype(jnp.float32)[:, None] * freqs[None, :]
    return (jnp.cos(angles)[:, None, :], jnp.sin(angles)[:, None, :])

def apply_rotary(value_rows, cosine_table, sine_table):
    half = HEAD_SIZE // 2
    first = value_rows[..., :half]
    second = value_rows[..., half:]
    return jnp.concatenate([first * cosine_table - second * sine_table, second * cosine_table + first * sine_table], axis=-1)

def attend_blocks(query_rows, key_rows, value_rows, token_positions):
    overall_rows = query_rows.shape[0]
    model_width = min(512, overall_rows)
    score_scale = HEAD_SIZE ** (-0.5)

    def one_block(index):
        begin = (index * model_width).astype(jnp.int32)
        block_attention = lax.dynamic_slice_in_dim(query_rows, begin, model_width, 0)
        block_places = lax.dynamic_slice_in_dim(token_positions, begin, model_width, 0)
        scores = lower_half_backward(jnp.einsum('qkgd,skd->kgqs', block_attention, key_rows, precision=HIGH) * score_scale)
        visible = token_positions[None, :] <= block_places[:, None]
        scores = jnp.where(visible, scores, SCORE_FLOOR)
        top = lax.optimization_barrier(jnp.max(scores, axis=-1, keepdims=True))
        weights = jnp.where(visible, jnp.exp(scores - top), 0.0)
        probs = lower_half(weights / lax.optimization_barrier(jnp.sum(weights, axis=-1, keepdims=True)))
        return jnp.einsum('kgqs,skd->qkgd', probs, value_rows, precision=HIGH)
    blocks = lax.map(jax.checkpoint(one_block), jnp.arange(overall_rows // model_width, dtype=jnp.int32))
    return blocks.reshape(overall_rows, QUERY_HEADS * HEAD_SIZE)

def layer(hidden, token_positions, query_w, key_matrix, value_w, output_matrix, gate_w, up_w, down_w, attn_gain, mlp_gain):
    overall_rows = hidden.shape[0]
    cosine_table, sine_table = rope_tables(token_positions)
    normalized_rows = lower_half(rms_scale(hidden, attn_gain))
    query_rows = lower_half_backward(jnp.dot(normalized_rows, query_w, precision=HIGH))
    key_rows = lower_half_backward(jnp.dot(normalized_rows, key_matrix, precision=HIGH))
    value_rows = lower_half(lower_half_backward(jnp.dot(normalized_rows, value_w, precision=HIGH)))
    query_rows = lower_half(apply_rotary(query_rows.reshape(overall_rows, QUERY_HEADS, HEAD_SIZE), cosine_table, sine_table))
    query_rows = query_rows.reshape(overall_rows, KEY_VALUE_HEADS, QUERY_HEADS // KEY_VALUE_HEADS, HEAD_SIZE)
    key_rows = lower_half(apply_rotary(key_rows.reshape(overall_rows, KEY_VALUE_HEADS, HEAD_SIZE), cosine_table, sine_table))
    mixed_heads = lower_half(lower_half_backward(attend_blocks(query_rows, key_rows, value_rows.reshape(overall_rows, KEY_VALUE_HEADS, HEAD_SIZE), token_positions)))
    middle = hidden + lower_half_backward(jnp.dot(mixed_heads, output_matrix, precision=HIGH))
    normed_mlp = lower_half(rms_scale(middle, mlp_gain))
    gate = lower_half_backward(jnp.dot(normed_mlp, gate_w, precision=HIGH))
    upward = lower_half_backward(jnp.dot(normed_mlp, up_w, precision=HIGH))
    inner = lower_half(jax.nn.silu(gate) * upward)
    return middle + lower_half_backward(jnp.dot(inner, down_w, precision=HIGH))

def reference(tokens, positions, cotangent, w_query, w_key, w_value, w_out, w_gate, w_up, w_down, gain_attn, gain_mlp):
    params = tuple((item.astype(jnp.float32) for item in (w_query, w_key, w_value, w_out, w_gate, w_up, w_down, gain_attn, gain_mlp)))

    def forward(weights, hidden, token_positions):
        for index in range(LAYERS):
            hidden = layer(hidden, token_positions, *[item[index] for item in weights])
        return hidden

    def one_sequence(carry, inputs):
        start, token_positions, upstream = inputs
        result, pull = jax.vjp(lambda weights, hidden: forward(weights, hidden, token_positions), params, start.astype(jnp.float32))
        grads, grad_input = pull(upstream.astype(jnp.float32))
        carry = jax.tree.map(lambda first, second: first + second, carry, grads)
        return (carry, (result.astype(jnp.bfloat16), grad_input.astype(jnp.bfloat16)))
    zero_filled = tuple((jnp.zeros(item.shape, jnp.float32) for item in params))
    sums, (results, grad_inputs) = lax.scan(one_sequence, zero_filled, (tokens, positions, cotangent))
    return (results, grad_inputs, sums[0], sums[1], sums[2], sums[3], sums[4], sums[5], sums[6], sums[7], sums[8])
```

```python
import functools

import jax
import jax.numpy as jnp
from jax import lax
from jax.experimental import pallas as pl
from jax.experimental.pallas import tpu as pltpu
from jax.sharding import PartitionSpec as P

QUERY_HEADS = 15
KEY_VALUE_HEADS = 5
HEAD_SIZE = 64
GROUP = QUERY_HEADS // KEY_VALUE_HEADS
QW = QUERY_HEADS * HEAD_SIZE
KVW = KEY_VALUE_HEADS * HEAD_SIZE
PAIR = 2 * KVW
BLK = 64
LANES = 128

EPS = 1e-05
ROPE_BASE = 100000.0
SCORE_FLOOR = -1e30
SCALE = HEAD_SIZE ** (-0.5)


def rope_tables(token_positions):
    half = HEAD_SIZE // 2
    freqs = ROPE_BASE ** (-jnp.arange(half, dtype=jnp.float32) * 2.0 / HEAD_SIZE)
    angles = token_positions.astype(jnp.float32)[:, None] * freqs[None, :]
    cosine, sine = jnp.cos(angles), jnp.sin(angles)
    return (
        jnp.concatenate([cosine, cosine], axis=1),
        jnp.concatenate([-sine, sine], axis=1),
    )


def swap_halves(rows):
    half = HEAD_SIZE // 2
    width = rows.shape[1]
    left = jnp.concatenate([rows[:, half:], rows[:, :half]], axis=1)
    right = jnp.concatenate([rows[:, width - half :], rows[:, : width - half]], axis=1)
    first = (lax.broadcasted_iota(jnp.int32, (1, width), 1) % HEAD_SIZE) < half
    return jnp.where(first, left, right)


def rotate(rows, cosine, sine):
    heads = rows.shape[1] // HEAD_SIZE
    return rows * jnp.tile(cosine, (1, heads)) + swap_halves(rows) * jnp.tile(sine, (1, heads))


def rms_factor(hidden):
    return lax.rsqrt(jnp.mean(hidden * hidden, axis=-1, keepdims=True) + EPS)


def norm_back(hidden, gain, grad_out):
    factor = rms_factor(hidden)
    scaled = grad_out * gain
    grad_gain = jnp.sum(grad_out * hidden * factor, axis=0)
    inner = jnp.mean(hidden * scaled, axis=-1, keepdims=True)
    return (factor * scaled - hidden * (factor * factor * factor) * inner, grad_gain)


def dot(left, right):
    return jnp.dot(left, right, preferred_element_type=jnp.float32)


def dot_t(left, right):
    return lax.dot_general(
        left, right, (((1,), (1,)), ((), ())), preferred_element_type=jnp.float32
    )


def t_dot(left, right):
    return lax.dot_general(
        left, right, (((0,), (0,)), ((), ())), preferred_element_type=jnp.float32
    )


def head_of(rows, index):
    return rows[:, index * HEAD_SIZE : (index + 1) * HEAD_SIZE]


def group_rows(ref, group):
    rows = ref[:, group * GROUP * HEAD_SIZE : (group + 1) * GROUP * HEAD_SIZE]
    return jnp.concatenate([head_of(rows, index) for index in range(GROUP)], axis=0)


def softmax_parts(query, key, visible):
    scores = jnp.where(visible, dot_t(query, key) * SCALE, SCORE_FLOOR)
    top = jnp.max(scores, axis=-1, keepdims=True)
    weights = jnp.where(visible, jnp.exp(scores - top), 0.0)
    return weights, jnp.sum(weights, axis=-1, keepdims=True)


def attend_kernel(query_ref, pair_ref, query_place_ref, key_place_ref, mixed_ref):
    tokens = query_ref.shape[0]
    visible = key_place_ref[...] <= query_place_ref[...]
    visible = jnp.concatenate([visible.astype(jnp.float32)] * GROUP, axis=0) > 0.5
    for group in range(KEY_VALUE_HEADS):
        key = pair_ref[:, group * HEAD_SIZE : (group + 1) * HEAD_SIZE]
        value = pair_ref[:, KVW + group * HEAD_SIZE : KVW + (group + 1) * HEAD_SIZE]
        weights, total = softmax_parts(group_rows(query_ref, group), key, visible)
        mixed = dot(weights.astype(jnp.bfloat16), value) / total
        mixed_ref[:, group * GROUP * HEAD_SIZE : (group + 1) * GROUP * HEAD_SIZE] = (
            jnp.concatenate(
                [mixed[index * tokens : (index + 1) * tokens] for index in range(GROUP)], axis=1
            )
        )


def attend_back_kernel(
    query_ref,
    pair_ref,
    query_place_ref,
    key_place_ref,
    mixed_ref,
    mixed_grad_ref,
    query_grad_ref,
    pair_grad_ref,
):
    tokens = query_ref.shape[0]
    visible = key_place_ref[...] <= query_place_ref[...]
    visible = jnp.concatenate([visible.astype(jnp.float32)] * GROUP, axis=0) > 0.5
    for group in range(KEY_VALUE_HEADS):
        key_at = slice(group * HEAD_SIZE, (group + 1) * HEAD_SIZE)
        value_at = slice(KVW + group * HEAD_SIZE, KVW + (group + 1) * HEAD_SIZE)
        key = pair_ref[:, key_at]
        value = pair_ref[:, value_at]
        query = group_rows(query_ref, group)
        mixed_grad = group_rows(mixed_grad_ref, group)
        delta = jnp.sum(
            mixed_grad.astype(jnp.float32) * group_rows(mixed_ref, group), axis=-1, keepdims=True
        )
        weights, total = softmax_parts(query, key, visible)
        probs = weights / total
        pair_grad_ref[:, value_at] = t_dot(probs.astype(jnp.bfloat16), mixed_grad).astype(
            jnp.bfloat16
        )
        grad_scores = (probs * (dot_t(mixed_grad, value) - delta)).astype(jnp.bfloat16)
        pair_grad_ref[:, key_at] = (t_dot(grad_scores, query) * SCALE).astype(jnp.bfloat16)
        query_grad = dot(grad_scores, key) * SCALE
        query_grad_ref[:, group * GROUP * HEAD_SIZE : (group + 1) * GROUP * HEAD_SIZE] = (
            jnp.concatenate(
                [query_grad[index * tokens : (index + 1) * tokens] for index in range(GROUP)],
                axis=1,
            )
        )


def kernel_call(kernel, outs, flops):
    return pl.pallas_call(
        kernel,
        out_shape=outs,
        compiler_params=pltpu.CompilerParams(vmem_limit_bytes=48 * 1024 * 1024),
        cost_estimate=pl.CostEstimate(flops=flops, bytes_accessed=6_000_000, transcendentals=0),
    )


def attend(query, pairs, query_place, key_place):
    tokens, keys = query.shape[0], pairs.shape[0]
    return kernel_call(
        attend_kernel,
        jax.ShapeDtypeStruct((tokens, QW), jnp.float32),
        4 * tokens * keys * QW * 4,
    )(query, pairs, query_place, key_place)


def attend_back(query, pairs, query_place, key_place, mixed, mixed_grad):
    tokens, keys = query.shape[0], pairs.shape[0]
    return kernel_call(
        attend_back_kernel,
        (
            jax.ShapeDtypeStruct((tokens, QW), jnp.float32),
            jax.ShapeDtypeStruct((keys, PAIR), jnp.bfloat16),
        ),
        10 * tokens * keys * QW * 4,
    )(query, pairs, query_place, key_place, mixed, mixed_grad)


def gather(item, axis_name):
    return lax.all_gather(item, axis_name, axis=0, tiled=True)


def scatter_sum(item, axis_name):
    return lax.psum_scatter(item, axis_name, scatter_dimension=0, tiled=True)


def on_device(
    tokens,
    positions,
    cotangent,
    w_query,
    w_key,
    w_value,
    w_out,
    w_gate,
    w_up,
    w_down,
    gain_attn,
    gain_mlp,
):
    layers, rows, width = w_query.shape[0], w_query.shape[1], w_query.shape[2]
    split = lax.axis_size("fsdp")
    ff_part = w_down.shape[1]
    low = jnp.bfloat16
    token_positions = positions[0]
    token_rows = token_positions.shape[0]
    cosine, sine = rope_tables(token_positions)
    query_place = token_positions[:, None]

    attn_parts = [
        gather(
            jnp.concatenate([w_query[l], w_key[l], w_value[l], w_out[l]], axis=1), "fsdp"
        )
        for l in range(layers)
    ]
    gains = lax.all_gather(jnp.concatenate([gain_attn, gain_mlp], axis=0), "fsdp", axis=1, tiled=True)
    attn_gains, mlp_gains = gains[:layers], gains[layers:]

    def columns(l):
        pieces = jnp.stack(
            [
                jnp.concatenate(
                    [
                        w_gate[l][:, part * ff_part : (part + 1) * ff_part],
                        w_up[l][:, part * ff_part : (part + 1) * ff_part],
                    ],
                    axis=1,
                )
                for part in range(split)
            ]
        )
        return lax.all_to_all(pieces, "fsdp", 0, 0, tiled=True).reshape(
            split * rows, 2 * ff_part
        )

    gate_up = [columns(l) for l in range(layers)]

    hidden = tokens[0].astype(jnp.float32)
    saved = []
    key_place = None
    for l in range(layers):
        w_qkv = attn_parts[l][:, : QW + PAIR]
        w_o = attn_parts[l][:, QW + PAIR :]
        normed = (hidden * rms_factor(hidden) * attn_gains[l]).astype(low)
        qkv = dot(normed, w_qkv)
        rotated = rotate(qkv[:, : QW + KVW], cosine, sine)
        query = rotated[:, :QW].astype(low)
        pairs = jnp.concatenate([rotated[:, QW:], qkv[:, QW + KVW :]], axis=1).astype(low)
        if key_place is None:
            places = jnp.stack([token_positions // BLK, token_positions % BLK], axis=1)
            places = jnp.pad(places.astype(low), ((0, 0), (0, LANES - 2)))
            all_pairs = gather(jnp.concatenate([pairs, places], axis=1), "ctx")
            key_place = (
                all_pairs[:, PAIR].astype(jnp.int32) * BLK
                + all_pairs[:, PAIR + 1].astype(jnp.int32)
            )[None, :]
            all_pairs = all_pairs[:, :PAIR]
        else:
            all_pairs = gather(pairs, "ctx")
        mixed = attend(query, all_pairs, query_place, key_place)
        mixed_low = mixed.astype(low)
        middle = hidden + dot(mixed_low, w_o)
        normed_mlp = gather((middle * rms_factor(middle) * mlp_gains[l]).astype(low), "fsdp")
        gate_and_up = dot(normed_mlp, gate_up[l])
        gate, up = gate_and_up[:, :ff_part], gate_and_up[:, ff_part:]
        inner = (jax.nn.silu(gate) * up).astype(low)
        saved.append(
            (hidden, normed, query, all_pairs, mixed, mixed_low, middle, normed_mlp, gate, up, inner)
        )
        hidden = middle + scatter_sum(dot(inner, w_down[l]).astype(low), "fsdp").astype(jnp.float32)
    output = hidden.astype(low)[None]

    grad = cotangent[0].astype(jnp.float32)
    collected = [None] * layers
    for l in reversed(range(layers)):
        (hidden, normed, query, all_pairs, mixed, mixed_low, middle, normed_mlp, gate, up, inner) = (
            saved[l]
        )
        w_qkv = attn_parts[l][:, : QW + PAIR]
        w_o = attn_parts[l][:, QW + PAIR :]
        grad_low = gather(grad.astype(low), "fsdp")
        grad_down = t_dot(inner, grad_low).astype(low)
        grad_inner = dot_t(grad_low, w_down[l])
        sigma = jax.nn.sigmoid(gate)
        d_up = (grad_inner * gate * sigma).astype(low)
        d_gate = (grad_inner * up * sigma * (1.0 + gate * (1.0 - sigma))).astype(low)
        d_both = jnp.concatenate([d_gate, d_up], axis=1)
        grad_normed_mlp = scatter_sum(dot_t(d_both, gate_up[l]).astype(low), "fsdp")
        grad_gate_up = t_dot(normed_mlp, d_both).astype(low)
        grad_middle, grad_mlp_gain = norm_back(
            middle, mlp_gains[l].astype(jnp.float32), grad_normed_mlp.astype(jnp.float32)
        )
        grad_middle = grad_middle + grad
        branch_low = grad_middle.astype(low)
        grad_out = t_dot(mixed_low, branch_low).astype(low)
        mixed_grad = dot_t(branch_low, w_o).astype(low)
        query_grad, pair_terms = attend_back(
            query, all_pairs, query_place, key_place, mixed, mixed_grad
        )
        pair_grad = scatter_sum(pair_terms, "ctx").astype(jnp.float32)
        qk_grad = rotate(
            jnp.concatenate([query_grad, pair_grad[:, :KVW]], axis=1), cosine, -sine
        )
        qkv_grad = jnp.concatenate([qk_grad, pair_grad[:, KVW:]], axis=1).astype(low)
        grad_qkv = t_dot(normed, qkv_grad).astype(low)
        grad_normed = dot_t(qkv_grad, w_qkv)
        grad_hidden, grad_attn_gain = norm_back(
            hidden, attn_gains[l].astype(jnp.float32), grad_normed
        )
        grad = grad_hidden + grad_middle
        exchanged = lax.all_to_all(
            grad_gate_up.reshape(split, rows, 2 * ff_part), "fsdp", 0, 0, tiled=True
        )
        exchanged = exchanged.reshape(split * rows, 2 * ff_part)
        attn_grads = scatter_sum(jnp.concatenate([grad_qkv, grad_out], axis=1), "fsdp")
        mlp_sum = lax.psum(exchanged, "ctx").reshape(split, rows, 2 * ff_part)
        down_sum = lax.psum(grad_down, "ctx")
        attn_sum = lax.psum(attn_grads, "ctx")
        collected[l] = (
            attn_sum[:, :QW],
            attn_sum[:, QW : QW + KVW],
            attn_sum[:, QW + KVW : QW + PAIR],
            attn_sum[:, QW + PAIR :],
            jnp.concatenate([mlp_sum[part, :, :ff_part] for part in range(split)], axis=1),
            jnp.concatenate([mlp_sum[part, :, ff_part:] for part in range(split)], axis=1),
            down_sum,
            grad_attn_gain,
            grad_mlp_gain,
        )
    grad_tokens = grad.astype(low)[None]
    gain_sums = scatter_sum(
        jnp.stack([collected[l][at] for at in (7, 8) for l in range(layers)], axis=1), "fsdp"
    )
    gain_sums = lax.psum(gain_sums, "ctx").T
    stacked = [
        jnp.stack([collected[l][member].astype(jnp.float32) for l in range(layers)])
        for member in range(7)
    ]
    return (output, grad_tokens, *stacked, gain_sums[:layers], gain_sums[layers:])


def solution(mesh):
    rows = P("fsdp", "ctx", None)
    weight = P(None, "fsdp", None)
    gain = P(None, "fsdp")
    return jax.shard_map(
        on_device,
        mesh=mesh,
        in_specs=(rows, P("fsdp", "ctx"), rows) + (weight,) * 7 + (gain,) * 2,
        out_specs=(rows, rows) + (weight,) * 7 + (gain,) * 2,
        check_vma=False,
    )
```

```python
import functools

import jax
import jax.numpy as jnp
from jax import lax
from jax.experimental import pallas as pl
from jax.experimental.pallas import tpu as pltpu
from jax.sharding import PartitionSpec as P

QUERY_HEADS = 15
KEY_VALUE_HEADS = 5
HEAD_SIZE = 64
GROUP = QUERY_HEADS // KEY_VALUE_HEADS
QW = QUERY_HEADS * HEAD_SIZE
KVW = KEY_VALUE_HEADS * HEAD_SIZE
PAIR = 2 * KVW
BLK = 64
LANES = 128

EPS = 1e-05
ROPE_BASE = 100000.0
SCORE_FLOOR = -1e30
SCALE = HEAD_SIZE ** (-0.5)


def rope_tables(token_positions):
    half = HEAD_SIZE // 2
    freqs = ROPE_BASE ** (-jnp.arange(half, dtype=jnp.float32) * 2.0 / HEAD_SIZE)
    angles = token_positions.astype(jnp.float32)[:, None] * freqs[None, :]
    cosine, sine = jnp.cos(angles), jnp.sin(angles)
    return (
        jnp.concatenate([cosine, cosine], axis=1),
        jnp.concatenate([-sine, sine], axis=1),
    )


def swap_halves(rows):
    half = HEAD_SIZE // 2
    width = rows.shape[1]
    left = jnp.concatenate([rows[:, half:], rows[:, :half]], axis=1)
    right = jnp.concatenate([rows[:, width - half :], rows[:, : width - half]], axis=1)
    first = (lax.broadcasted_iota(jnp.int32, (1, width), 1) % HEAD_SIZE) < half
    return jnp.where(first, left, right)


def rotate(rows, cosine, sine):
    heads = rows.shape[1] // HEAD_SIZE
    return rows * jnp.tile(cosine, (1, heads)) + swap_halves(rows) * jnp.tile(sine, (1, heads))


def rms_factor(hidden):
    return lax.rsqrt(jnp.mean(hidden * hidden, axis=-1, keepdims=True) + EPS)


def norm_back(hidden, gain, grad_out):
    factor = rms_factor(hidden)
    scaled = grad_out * gain
    grad_gain = jnp.sum(grad_out * hidden * factor, axis=0)
    inner = jnp.mean(hidden * scaled, axis=-1, keepdims=True)
    return (factor * scaled - hidden * (factor * factor * factor) * inner, grad_gain)


def dot(left, right):
    return jnp.dot(left, right, preferred_element_type=jnp.float32)


def dot_t(left, right):
    return lax.dot_general(
        left, right, (((1,), (1,)), ((), ())), preferred_element_type=jnp.float32
    )


def t_dot(left, right):
    return lax.dot_general(
        left, right, (((0,), (0,)), ((), ())), preferred_element_type=jnp.float32
    )


def head_of(rows, index):
    return rows[:, index * HEAD_SIZE : (index + 1) * HEAD_SIZE]


def group_rows(ref, group):
    rows = ref[:, group * GROUP * HEAD_SIZE : (group + 1) * GROUP * HEAD_SIZE]
    return jnp.concatenate([head_of(rows, index) for index in range(GROUP)], axis=0)


def softmax_parts(query, key, visible):
    scores = jnp.where(visible, dot_t(query, key) * SCALE, SCORE_FLOOR)
    top = jnp.max(scores, axis=-1, keepdims=True)
    weights = jnp.where(visible, jnp.exp(scores - top), 0.0)
    return weights, jnp.sum(weights, axis=-1, keepdims=True)


def attend_kernel(query_ref, pair_ref, query_place_ref, key_place_ref, mixed_ref):
    tokens = query_ref.shape[0]
    visible = key_place_ref[...] <= query_place_ref[...]
    visible = jnp.concatenate([visible.astype(jnp.float32)] * GROUP, axis=0) > 0.5
    for group in range(KEY_VALUE_HEADS):
        key = pair_ref[:, group * HEAD_SIZE : (group + 1) * HEAD_SIZE]
        value = pair_ref[:, KVW + group * HEAD_SIZE : KVW + (group + 1) * HEAD_SIZE]
        weights, total = softmax_parts(group_rows(query_ref, group), key, visible)
        mixed = dot(weights.astype(jnp.bfloat16), value) / total
        mixed_ref[:, group * GROUP * HEAD_SIZE : (group + 1) * GROUP * HEAD_SIZE] = (
            jnp.concatenate(
                [mixed[index * tokens : (index + 1) * tokens] for index in range(GROUP)], axis=1
            )
        )


def attend_back_kernel(
    query_ref,
    pair_ref,
    query_place_ref,
    key_place_ref,
    mixed_ref,
    mixed_grad_ref,
    query_grad_ref,
    pair_grad_ref,
):
    tokens = query_ref.shape[0]
    visible = key_place_ref[...] <= query_place_ref[...]
    visible = jnp.concatenate([visible.astype(jnp.float32)] * GROUP, axis=0) > 0.5
    for group in range(KEY_VALUE_HEADS):
        key_at = slice(group * HEAD_SIZE, (group + 1) * HEAD_SIZE)
        value_at = slice(KVW + group * HEAD_SIZE, KVW + (group + 1) * HEAD_SIZE)
        key = pair_ref[:, key_at]
        value = pair_ref[:, value_at]
        query = group_rows(query_ref, group)
        mixed_grad = group_rows(mixed_grad_ref, group)
        delta = jnp.sum(
            mixed_grad.astype(jnp.float32) * group_rows(mixed_ref, group), axis=-1, keepdims=True
        )
        weights, total = softmax_parts(query, key, visible)
        probs = weights / total
        pair_grad_ref[:, value_at] = t_dot(probs.astype(jnp.bfloat16), mixed_grad).astype(
            jnp.bfloat16
        )
        grad_scores = (probs * (dot_t(mixed_grad, value) - delta)).astype(jnp.bfloat16)
        pair_grad_ref[:, key_at] = (t_dot(grad_scores, query) * SCALE).astype(jnp.bfloat16)
        query_grad = dot(grad_scores, key) * SCALE
        query_grad_ref[:, group * GROUP * HEAD_SIZE : (group + 1) * GROUP * HEAD_SIZE] = (
            jnp.concatenate(
                [query_grad[index * tokens : (index + 1) * tokens] for index in range(GROUP)],
                axis=1,
            )
        )


def kernel_call(kernel, outs, flops):
    return pl.pallas_call(
        kernel,
        out_shape=outs,
        compiler_params=pltpu.CompilerParams(vmem_limit_bytes=48 * 1024 * 1024),
        cost_estimate=pl.CostEstimate(flops=flops, bytes_accessed=6_000_000, transcendentals=0),
    )


def attend(query, pairs, query_place, key_place):
    tokens, keys = query.shape[0], pairs.shape[0]
    return kernel_call(
        attend_kernel,
        jax.ShapeDtypeStruct((tokens, QW), jnp.float32),
        4 * tokens * keys * QW * 4,
    )(query, pairs, query_place, key_place)


def attend_back(query, pairs, query_place, key_place, mixed, mixed_grad):
    tokens, keys = query.shape[0], pairs.shape[0]
    return kernel_call(
        attend_back_kernel,
        (
            jax.ShapeDtypeStruct((tokens, QW), jnp.float32),
            jax.ShapeDtypeStruct((keys, PAIR), jnp.bfloat16),
        ),
        10 * tokens * keys * QW * 4,
    )(query, pairs, query_place, key_place, mixed, mixed_grad)


def gather(item, axis_name):
    return lax.all_gather(item, axis_name, axis=0, tiled=True)


def scatter_sum(item, axis_name):
    return lax.psum_scatter(item, axis_name, scatter_dimension=0, tiled=True)


def exchange_sum(item, axis_name):
    parts = lax.axis_size(axis_name)
    blocks = item.reshape(parts, item.shape[0] // parts, item.shape[1])
    blocks = lax.all_to_all(blocks, axis_name, 0, 0, tiled=True)
    return jnp.sum(blocks.astype(jnp.float32), axis=0)


def together(*items):
    return lax.optimization_barrier(items)


def on_device(
    tokens,
    positions,
    cotangent,
    w_query,
    w_key,
    w_value,
    w_out,
    w_gate,
    w_up,
    w_down,
    gain_attn,
    gain_mlp,
):
    layers, rows, width = w_query.shape[0], w_query.shape[1], w_query.shape[2]
    split = lax.axis_size("fsdp")
    ff_part = w_down.shape[1]
    low = jnp.bfloat16
    token_positions = positions[0]
    token_rows = token_positions.shape[0]
    cosine, sine = rope_tables(token_positions)
    query_place = token_positions[:, None]

    attn_parts = [
        gather(
            jnp.concatenate([w_query[l], w_key[l], w_value[l], w_out[l]], axis=1), "fsdp"
        )
        for l in range(layers)
    ]
    gains = lax.all_gather(jnp.concatenate([gain_attn, gain_mlp], axis=0), "fsdp", axis=1, tiled=True)
    attn_gains, mlp_gains = gains[:layers], gains[layers:]

    def columns(l):
        pieces = jnp.stack(
            [
                jnp.concatenate(
                    [
                        w_gate[l][:, part * ff_part : (part + 1) * ff_part],
                        w_up[l][:, part * ff_part : (part + 1) * ff_part],
                    ],
                    axis=1,
                )
                for part in range(split)
            ]
        )
        return lax.all_to_all(pieces, "fsdp", 0, 0, tiled=True).reshape(
            split * rows, 2 * ff_part
        )

    gate_up = [columns(l) for l in range(layers)]

    hidden = tokens[0].astype(jnp.float32)
    saved = []
    key_place = None
    for l in range(layers):
        w_qkv = attn_parts[l][:, : QW + PAIR]
        w_o = attn_parts[l][:, QW + PAIR :]
        normed = (hidden * rms_factor(hidden) * attn_gains[l]).astype(low)
        qkv = dot(normed, w_qkv)
        rotated = rotate(qkv[:, : QW + KVW], cosine, sine)
        query = rotated[:, :QW].astype(low)
        pairs = jnp.concatenate([rotated[:, QW:], qkv[:, QW + KVW :]], axis=1).astype(low)
        if key_place is None:
            places = jnp.stack([token_positions // BLK, token_positions % BLK], axis=1)
            places = jnp.pad(places.astype(low), ((0, 0), (0, LANES - 2)))
            all_pairs = gather(jnp.concatenate([pairs, places], axis=1), "ctx")
            key_place = (
                all_pairs[:, PAIR].astype(jnp.int32) * BLK
                + all_pairs[:, PAIR + 1].astype(jnp.int32)
            )[None, :]
            all_pairs = all_pairs[:, :PAIR]
        else:
            all_pairs = gather(pairs, "ctx")
        mixed = attend(query, all_pairs, query_place, key_place)
        mixed_low = mixed.astype(low)
        middle = hidden + dot(mixed_low, w_o)
        normed_mlp = gather((middle * rms_factor(middle) * mlp_gains[l]).astype(low), "fsdp")
        if l + 1 < layers:
            normed_mlp, attn_parts[l + 1] = together(normed_mlp, attn_parts[l + 1])
        gate_and_up = dot(normed_mlp, gate_up[l])
        gate, up = gate_and_up[:, :ff_part], gate_and_up[:, ff_part:]
        inner = (jax.nn.silu(gate) * up).astype(low)
        saved.append(
            (hidden, normed, query, all_pairs, mixed, mixed_low, middle, normed_mlp, gate, up, inner)
        )
        partial = dot(inner, w_down[l]).astype(low)
        if l + 1 < layers:
            partial, gate_up[l + 1] = together(partial, gate_up[l + 1])
        hidden = middle + exchange_sum(partial, "fsdp")
    output = hidden.astype(low)[None]

    grad = cotangent[0].astype(jnp.float32)
    waiting, mlp_sums, attn_sums, gain_grads = None, [], [], []
    for l in reversed(range(layers)):
        (hidden, normed, query, all_pairs, mixed, mixed_low, middle, normed_mlp, gate, up, inner) = (
            saved[l]
        )
        w_qkv = attn_parts[l][:, : QW + PAIR]
        w_o = attn_parts[l][:, QW + PAIR :]
        grad_low = gather(grad.astype(low), "fsdp")
        grad_down = t_dot(inner, grad_low).astype(low)
        grad_inner = dot_t(grad_low, w_down[l])
        sigma = jax.nn.sigmoid(gate)
        d_up = (grad_inner * gate * sigma).astype(low)
        d_gate = (grad_inner * up * sigma * (1.0 + gate * (1.0 - sigma))).astype(low)
        d_both = jnp.concatenate([d_gate, d_up], axis=1)
        grad_normed_mlp = exchange_sum(dot_t(d_both, gate_up[l]).astype(low), "fsdp")
        grad_gate_up = t_dot(normed_mlp, d_both).astype(low)
        exchanged = lax.all_to_all(
            grad_gate_up.reshape(split, rows, 2 * ff_part), "fsdp", 0, 0, tiled=True
        )
        exchanged = exchanged.reshape(split * rows, 2 * ff_part)
        grad_middle, grad_mlp_gain = norm_back(
            middle, mlp_gains[l].astype(jnp.float32), grad_normed_mlp
        )
        grad_middle = grad_middle + grad
        branch_low = grad_middle.astype(low)
        grad_out = t_dot(mixed_low, branch_low).astype(low)
        mixed_grad = dot_t(branch_low, w_o).astype(low)
        mixed_grad, exchanged, grad_down = together(mixed_grad, exchanged, grad_down)
        if waiting is None:
            mlp_sum, down_sum = lax.psum((exchanged, grad_down), "ctx")
        else:
            exchanged, grad_down, attn_grads, mlp_sums[-1] = together(
                exchanged, grad_down, waiting, mlp_sums[-1]
            )
            mlp_sum, down_sum, attn_sum = lax.psum((exchanged, grad_down, attn_grads), "ctx")
            attn_sums.append(attn_sum)
        mlp_sums.append((mlp_sum, down_sum))
        query_grad, pair_terms = attend_back(
            query, all_pairs, query_place, key_place, mixed, mixed_grad
        )
        pair_grad = exchange_sum(pair_terms, "ctx")
        qk_grad = rotate(
            jnp.concatenate([query_grad, pair_grad[:, :KVW]], axis=1), cosine, -sine
        )
        qkv_grad = jnp.concatenate([qk_grad, pair_grad[:, KVW:]], axis=1).astype(low)
        grad_qkv = t_dot(normed, qkv_grad).astype(low)
        grad_normed = dot_t(qkv_grad, w_qkv)
        grad_hidden, grad_attn_gain = norm_back(
            hidden, attn_gains[l].astype(jnp.float32), grad_normed
        )
        grad = grad_hidden + grad_middle
        waiting = scatter_sum(jnp.concatenate([grad_qkv, grad_out], axis=1), "fsdp")
        gain_grads = [(grad_attn_gain, grad_mlp_gain)] + gain_grads
    grad_tokens = grad.astype(low)[None]
    gain_sums = lax.psum(
        jnp.stack([pair[at] for at in (0, 1) for pair in gain_grads]), ("fsdp", "ctx")
    )
    gain_sums = lax.dynamic_slice_in_dim(gain_sums, lax.axis_index("fsdp") * rows, rows, 1)
    attn_grads, gain_sums, mlp_sums[-1] = together(waiting, gain_sums, mlp_sums[-1])
    attn_sums.append(lax.psum(attn_grads, "ctx"))
    collected = []
    for (mlp_sum, down_sum), attn_sum in zip(reversed(mlp_sums), reversed(attn_sums)):
        mlp_sum = mlp_sum.reshape(split, rows, 2 * ff_part)
        collected.append(
            (
                attn_sum[:, :QW],
                attn_sum[:, QW : QW + KVW],
                attn_sum[:, QW + KVW : QW + PAIR],
                attn_sum[:, QW + PAIR :],
                jnp.concatenate([mlp_sum[part, :, :ff_part] for part in range(split)], axis=1),
                jnp.concatenate([mlp_sum[part, :, ff_part:] for part in range(split)], axis=1),
                down_sum,
            )
        )
    stacked = [
        jnp.stack([collected[l][member].astype(jnp.float32) for l in range(layers)])
        for member in range(7)
    ]
    return (output, grad_tokens, *stacked, gain_sums[:layers], gain_sums[layers:])


def solution(mesh):
    rows = P("fsdp", "ctx", None)
    weight = P(None, "fsdp", None)
    gain = P(None, "fsdp")
    return jax.shard_map(
        on_device,
        mesh=mesh,
        in_specs=(rows, P("fsdp", "ctx"), rows) + (weight,) * 7 + (gain,) * 2,
        out_specs=(rows, rows) + (weight,) * 7 + (gain,) * 2,
        check_vma=False,
    )
```

```python
import functools

import jax
import jax.numpy as jnp
from jax import lax
from jax.experimental import pallas as pl
from jax.experimental.pallas import tpu as pltpu
from jax.sharding import PartitionSpec as P

QUERY_HEADS = 15
KEY_VALUE_HEADS = 5
HEAD_SIZE = 64
GROUP = QUERY_HEADS // KEY_VALUE_HEADS
QW = QUERY_HEADS * HEAD_SIZE
KVW = KEY_VALUE_HEADS * HEAD_SIZE
PAIR = 2 * KVW
BLK = 64
LANES = 128

EPS = 1e-05
ROPE_BASE = 100000.0
SCORE_FLOOR = -1e30
SCALE = HEAD_SIZE ** (-0.5)


def rope_tables(token_positions):
    half = HEAD_SIZE // 2
    freqs = ROPE_BASE ** (-jnp.arange(half, dtype=jnp.float32) * 2.0 / HEAD_SIZE)
    angles = token_positions.astype(jnp.float32)[:, None] * freqs[None, :]
    cosine, sine = jnp.cos(angles), jnp.sin(angles)
    return (
        jnp.concatenate([cosine, cosine], axis=1),
        jnp.concatenate([-sine, sine], axis=1),
    )


def swap_halves(rows):
    half = HEAD_SIZE // 2
    width = rows.shape[1]
    left = jnp.concatenate([rows[:, half:], rows[:, :half]], axis=1)
    right = jnp.concatenate([rows[:, width - half :], rows[:, : width - half]], axis=1)
    first = (lax.broadcasted_iota(jnp.int32, (1, width), 1) % HEAD_SIZE) < half
    return jnp.where(first, left, right)


def rotate(rows, cosine, sine):
    heads = rows.shape[1] // HEAD_SIZE
    return rows * jnp.tile(cosine, (1, heads)) + swap_halves(rows) * jnp.tile(sine, (1, heads))


def rms_factor(hidden):
    return lax.rsqrt(jnp.mean(hidden * hidden, axis=-1, keepdims=True) + EPS)


def norm_back(hidden, gain, grad_out):
    factor = rms_factor(hidden)
    scaled = grad_out * gain
    grad_gain = jnp.sum(grad_out * hidden * factor, axis=0)
    inner = jnp.mean(hidden * scaled, axis=-1, keepdims=True)
    return (factor * scaled - hidden * (factor * factor * factor) * inner, grad_gain)


def dot(left, right):
    return jnp.dot(left, right, preferred_element_type=jnp.float32)


def dot_t(left, right):
    return lax.dot_general(
        left, right, (((1,), (1,)), ((), ())), preferred_element_type=jnp.float32
    )


def t_dot(left, right):
    return lax.dot_general(
        left, right, (((0,), (0,)), ((), ())), preferred_element_type=jnp.float32
    )


def head_of(rows, index):
    return rows[:, index * HEAD_SIZE : (index + 1) * HEAD_SIZE]


def group_rows(ref, group):
    rows = ref[:, group * GROUP * HEAD_SIZE : (group + 1) * GROUP * HEAD_SIZE]
    return jnp.concatenate([head_of(rows, index) for index in range(GROUP)], axis=0)


def softmax_parts(query, key, visible):
    scores = jnp.where(visible, dot_t(query, key) * SCALE, SCORE_FLOOR)
    top = jnp.max(scores, axis=-1, keepdims=True)
    weights = jnp.where(visible, jnp.exp(scores - top), 0.0)
    return weights, jnp.sum(weights, axis=-1, keepdims=True)


def attend_kernel(query_ref, pair_ref, query_place_ref, key_place_ref, mixed_ref):
    tokens = query_ref.shape[0]
    visible = key_place_ref[...] <= query_place_ref[...]
    visible = jnp.concatenate([visible.astype(jnp.float32)] * GROUP, axis=0) > 0.5
    for group in range(KEY_VALUE_HEADS):
        key = pair_ref[:, group * HEAD_SIZE : (group + 1) * HEAD_SIZE]
        value = pair_ref[:, KVW + group * HEAD_SIZE : KVW + (group + 1) * HEAD_SIZE]
        weights, total = softmax_parts(group_rows(query_ref, group), key, visible)
        mixed = dot(weights.astype(jnp.bfloat16), value) / total
        mixed_ref[:, group * GROUP * HEAD_SIZE : (group + 1) * GROUP * HEAD_SIZE] = (
            jnp.concatenate(
                [mixed[index * tokens : (index + 1) * tokens] for index in range(GROUP)], axis=1
            )
        )


def attend_back_kernel(
    query_ref,
    pair_ref,
    query_place_ref,
    key_place_ref,
    mixed_ref,
    mixed_grad_ref,
    query_grad_ref,
    pair_grad_ref,
):
    tokens = query_ref.shape[0]
    visible = key_place_ref[...] <= query_place_ref[...]
    visible = jnp.concatenate([visible.astype(jnp.float32)] * GROUP, axis=0) > 0.5
    for group in range(KEY_VALUE_HEADS):
        key_at = slice(group * HEAD_SIZE, (group + 1) * HEAD_SIZE)
        value_at = slice(KVW + group * HEAD_SIZE, KVW + (group + 1) * HEAD_SIZE)
        key = pair_ref[:, key_at]
        value = pair_ref[:, value_at]
        query = group_rows(query_ref, group)
        mixed_grad = group_rows(mixed_grad_ref, group)
        delta = jnp.sum(
            mixed_grad.astype(jnp.float32) * group_rows(mixed_ref, group), axis=-1, keepdims=True
        )
        weights, total = softmax_parts(query, key, visible)
        probs = weights / total
        pair_grad_ref[:, value_at] = t_dot(probs.astype(jnp.bfloat16), mixed_grad).astype(
            jnp.bfloat16
        )
        grad_scores = (probs * (dot_t(mixed_grad, value) - delta)).astype(jnp.bfloat16)
        pair_grad_ref[:, key_at] = (t_dot(grad_scores, query) * SCALE).astype(jnp.bfloat16)
        query_grad = dot(grad_scores, key) * SCALE
        query_grad_ref[:, group * GROUP * HEAD_SIZE : (group + 1) * GROUP * HEAD_SIZE] = (
            jnp.concatenate(
                [query_grad[index * tokens : (index + 1) * tokens] for index in range(GROUP)],
                axis=1,
            )
        )


def kernel_call(kernel, outs, flops):
    return pl.pallas_call(
        kernel,
        out_shape=outs,
        compiler_params=pltpu.CompilerParams(vmem_limit_bytes=48 * 1024 * 1024),
        cost_estimate=pl.CostEstimate(flops=flops, bytes_accessed=6_000_000, transcendentals=0),
    )


def attend(query, pairs, query_place, key_place):
    tokens, keys = query.shape[0], pairs.shape[0]
    return kernel_call(
        attend_kernel,
        jax.ShapeDtypeStruct((tokens, QW), jnp.float32),
        4 * tokens * keys * QW * 4,
    )(query, pairs, query_place, key_place)


def attend_back(query, pairs, query_place, key_place, mixed, mixed_grad):
    tokens, keys = query.shape[0], pairs.shape[0]
    return kernel_call(
        attend_back_kernel,
        (
            jax.ShapeDtypeStruct((tokens, QW), jnp.float32),
            jax.ShapeDtypeStruct((keys, PAIR), jnp.bfloat16),
        ),
        10 * tokens * keys * QW * 4,
    )(query, pairs, query_place, key_place, mixed, mixed_grad)


def gather(item, axis_name):
    return lax.all_gather(item, axis_name, axis=0, tiled=True)


def scatter_sum(item, axis_name):
    return lax.psum_scatter(item, axis_name, scatter_dimension=0, tiled=True)


def exchange_sum(item, axis_name):
    parts = lax.axis_size(axis_name)
    blocks = item.reshape(parts, item.shape[0] // parts, item.shape[1])
    blocks = lax.all_to_all(blocks, axis_name, 0, 0, tiled=True)
    return jnp.sum(blocks.astype(jnp.float32), axis=0)


def together(*items):
    return lax.optimization_barrier(items)


def on_device(
    tokens,
    positions,
    cotangent,
    w_query,
    w_key,
    w_value,
    w_out,
    w_gate,
    w_up,
    w_down,
    gain_attn,
    gain_mlp,
):
    layers, rows, width = w_query.shape[0], w_query.shape[1], w_query.shape[2]
    split = lax.axis_size("fsdp")
    ff_part = w_down.shape[1]
    low = jnp.bfloat16
    token_positions = positions[0]
    token_rows = token_positions.shape[0]
    cosine, sine = rope_tables(token_positions)
    query_place = token_positions[:, None]

    attn_parts = [
        gather(
            jnp.concatenate([w_query[l], w_key[l], w_value[l], w_out[l]], axis=1), "fsdp"
        )
        for l in range(layers)
    ]
    gains = lax.all_gather(jnp.concatenate([gain_attn, gain_mlp], axis=0), "fsdp", axis=1, tiled=True)
    attn_gains, mlp_gains = gains[:layers], gains[layers:]

    def columns(l):
        pieces = jnp.stack(
            [
                jnp.concatenate(
                    [
                        w_gate[l][:, part * ff_part : (part + 1) * ff_part],
                        w_up[l][:, part * ff_part : (part + 1) * ff_part],
                    ],
                    axis=1,
                )
                for part in range(split)
            ]
        )
        return lax.all_to_all(pieces, "fsdp", 0, 0, tiled=True).reshape(
            split * rows, 2 * ff_part
        )

    gate_up = [columns(l) for l in range(layers)]

    hidden = tokens[0].astype(jnp.float32)
    saved = []
    key_place = None
    for l in range(layers):
        w_qkv = attn_parts[l][:, : QW + PAIR]
        w_o = attn_parts[l][:, QW + PAIR :]
        normed = (hidden * rms_factor(hidden) * attn_gains[l]).astype(low)
        qkv = dot(normed, w_qkv)
        rotated = rotate(qkv[:, : QW + KVW], cosine, sine)
        query = rotated[:, :QW].astype(low)
        pairs = jnp.concatenate([rotated[:, QW:], qkv[:, QW + KVW :]], axis=1).astype(low)
        if key_place is None:
            places = jnp.stack([token_positions // BLK, token_positions % BLK], axis=1)
            places = jnp.pad(places.astype(low), ((0, 0), (0, LANES - 2)))
            all_pairs = gather(jnp.concatenate([pairs, places], axis=1), "ctx")
            key_place = (
                all_pairs[:, PAIR].astype(jnp.int32) * BLK
                + all_pairs[:, PAIR + 1].astype(jnp.int32)
            )[None, :]
            all_pairs = all_pairs[:, :PAIR]
        else:
            all_pairs = gather(pairs, "ctx")
        mixed = attend(query, all_pairs, query_place, key_place)
        mixed_low = mixed.astype(low)
        middle = hidden + dot(mixed_low, w_o)
        normed_mlp = gather((middle * rms_factor(middle) * mlp_gains[l]).astype(low), "fsdp")
        if l + 1 < layers:
            normed_mlp, attn_parts[l + 1] = together(normed_mlp, attn_parts[l + 1])
        gate_and_up = dot(normed_mlp, gate_up[l])
        gate, up = gate_and_up[:, :ff_part], gate_and_up[:, ff_part:]
        inner = (jax.nn.silu(gate) * up).astype(low)
        saved.append(
            (hidden, normed, query, all_pairs, mixed, mixed_low, middle, normed_mlp, gate, up, inner)
        )
        partial = dot(inner, w_down[l]).astype(low)
        if l + 1 < layers:
            partial, gate_up[l + 1] = together(partial, gate_up[l + 1])
        hidden = middle + exchange_sum(partial, "fsdp")
    output = hidden.astype(low)[None]

    grad = cotangent[0].astype(jnp.float32)
    waiting, mlp_sums, attn_sums, gain_grads = None, [], [], []
    for l in reversed(range(layers)):
        (hidden, normed, query, all_pairs, mixed, mixed_low, middle, normed_mlp, gate, up, inner) = (
            saved[l]
        )
        w_qkv = attn_parts[l][:, : QW + PAIR]
        w_o = attn_parts[l][:, QW + PAIR :]
        grad_low = gather(grad.astype(low), "fsdp")
        grad_down = t_dot(inner, grad_low).astype(low)
        grad_inner = dot_t(grad_low, w_down[l])
        sigma = jax.nn.sigmoid(gate)
        d_up = (grad_inner * gate * sigma).astype(low)
        d_gate = (grad_inner * up * sigma * (1.0 + gate * (1.0 - sigma))).astype(low)
        d_both = jnp.concatenate([d_gate, d_up], axis=1)
        grad_normed_mlp = exchange_sum(dot_t(d_both, gate_up[l]).astype(low), "fsdp")
        grad_gate_up = t_dot(normed_mlp, d_both).astype(low)
        exchanged = lax.all_to_all(
            grad_gate_up.reshape(split, rows, 2 * ff_part), "fsdp", 0, 0, tiled=True
        )
        exchanged = exchanged.reshape(split * rows, 2 * ff_part)
        grad_middle, grad_mlp_gain = norm_back(
            middle, mlp_gains[l].astype(jnp.float32), grad_normed_mlp
        )
        grad_middle = grad_middle + grad
        branch_low = grad_middle.astype(low)
        grad_out = t_dot(mixed_low, branch_low).astype(low)
        mixed_grad = dot_t(branch_low, w_o).astype(low)
        mixed_grad, exchanged, grad_down = together(mixed_grad, exchanged, grad_down)
        if waiting is None:
            mlp_sum, down_sum = lax.psum((exchanged, grad_down), "ctx")
        else:
            exchanged, grad_down, attn_grads, mlp_sums[-1] = together(
                exchanged, grad_down, waiting, mlp_sums[-1]
            )
            mlp_sum, down_sum, attn_sum = lax.psum((exchanged, grad_down, attn_grads), "ctx")
            attn_sums.append(attn_sum)
        mlp_sums.append((mlp_sum, down_sum))
        query_grad, pair_terms = attend_back(
            query, all_pairs, query_place, key_place, mixed, mixed_grad
        )
        pair_grad = exchange_sum(pair_terms, "ctx")
        qk_grad = rotate(
            jnp.concatenate([query_grad, pair_grad[:, :KVW]], axis=1), cosine, -sine
        )
        qkv_grad = jnp.concatenate([qk_grad, pair_grad[:, KVW:]], axis=1).astype(low)
        grad_qkv = t_dot(normed, qkv_grad).astype(low)
        grad_normed = dot_t(qkv_grad, w_qkv)
        grad_hidden, grad_attn_gain = norm_back(
            hidden, attn_gains[l].astype(jnp.float32), grad_normed
        )
        grad = grad_hidden + grad_middle
        waiting = jnp.concatenate([grad_qkv, grad_out], axis=1)
        if l > 0:
            waiting = scatter_sum(waiting, "fsdp")
        else:
            waiting = exchange_sum(waiting, "fsdp").astype(low)
        gain_grads = [(grad_attn_gain, grad_mlp_gain)] + gain_grads
    grad_tokens = grad.astype(low)[None]
    gain_sums = lax.psum(
        jnp.stack([pair[at] for at in (0, 1) for pair in gain_grads]), ("fsdp", "ctx")
    )
    gain_sums = lax.dynamic_slice_in_dim(gain_sums, lax.axis_index("fsdp") * rows, rows, 1)
    attn_grads, gain_sums, mlp_sums[-1] = together(waiting, gain_sums, mlp_sums[-1])
    attn_sums.append(lax.psum(attn_grads, "ctx"))
    collected = []
    for (mlp_sum, down_sum), attn_sum in zip(reversed(mlp_sums), reversed(attn_sums)):
        mlp_sum = mlp_sum.reshape(split, rows, 2 * ff_part)
        collected.append(
            (
                attn_sum[:, :QW],
                attn_sum[:, QW : QW + KVW],
                attn_sum[:, QW + KVW : QW + PAIR],
                attn_sum[:, QW + PAIR :],
                jnp.concatenate([mlp_sum[part, :, :ff_part] for part in range(split)], axis=1),
                jnp.concatenate([mlp_sum[part, :, ff_part:] for part in range(split)], axis=1),
                down_sum,
            )
        )
    stacked = [
        jnp.stack([collected[l][member].astype(jnp.float32) for l in range(layers)])
        for member in range(7)
    ]
    return (output, grad_tokens, *stacked, gain_sums[:layers], gain_sums[layers:])


def solution(mesh):
    rows = P("fsdp", "ctx", None)
    weight = P(None, "fsdp", None)
    gain = P(None, "fsdp")
    return jax.shard_map(
        on_device,
        mesh=mesh,
        in_specs=(rows, P("fsdp", "ctx"), rows) + (weight,) * 7 + (gain,) * 2,
        out_specs=(rows, rows) + (weight,) * 7 + (gain,) * 2,
        check_vma=False,
    )
```
